32 devices in a mesh: dp: 32 (over z, y, x, core).
Axes of the slice: x: 2, y: 2, z: 4, core: 2. Of those that a mesh axis runs over, the one named last changes fastest.
Arguments:
- frames: bfloat16 [256, 16, 16, 128], P('dp'), may hold values from -6 to 6
- clip_blocks: int32 [4], replicated, may hold values from 1 to 16, 32 in all
- tail_frames: int32 [4], replicated, may hold values from 1 to 8
- weight_one: bfloat16 [3, 3, 3, 128, 128], replicated, may hold values from -0.109375 to 0.109375
- weight_two: bfloat16 [3, 3, 3, 128, 256], replicated, may hold values from -0.109375 to 0.109375
- cotangent: bfloat16 [256, 16, 16, 256], P('dp'), may hold values from -6 to 6
Outputs:
- features: bfloat16 [256, 16, 16, 256], P('dp')
- grad_one: float32 [3, 3, 3, 128, 128], replicated
- grad_two: float32 [3, 3, 3, 128, 256], replicated
The draws below stay inside these ranges and needn't reach their ends.
Inputs may be any that keep to these rules, and one draw needn't show every extreme that they name: `clip_blocks`: the blocks of all clips add up to 32; the longest clip has exactly 16 blocks.
All inputs are finite; a program needn't handle non-finite values.
Results may differ from the reference program's by a relative error of at most 0.005.
Values may be sent and summed in bfloat16 or wider, within the bound.
A program may use at most 64 MiB of HBM per device.

```python
import math
import jax
import jax.numpy as jnp
import numpy as np
from jax import lax

GROUP = 8
TILE_H = 16
TILE_W = 16
C_IN = 128
C_MID = 128
C_OUT = 256
CLIPS = 4
MOST = 16
FRAMES = 256
N_DP = 32


def set_ends(drawn, own_key, least, largest):
    spot = [jax.random.randint(jax.random.fold_in(own_key, axis), (), 0, length) for axis, length in enumerate(drawn.shape)]
    widest = drawn.shape.index(max(drawn.shape))
    beside = spot[:widest] + [(spot[widest] + 1) % drawn.shape[widest]] + spot[widest + 1:]
    return drawn.at[tuple(spot)].set(least).at[tuple(beside)].set(largest)


def block_scale(key, shape, shards, smallest, high):
    factor_of = 1.0
    for axis_at, blocks in shards:
        draws = jax.random.uniform(jax.random.fold_in(jax.random.fold_in(key, 6), axis_at), (blocks,), jnp.float32, smallest / len(shards), high / len(shards))
        factor_of = factor_of * jnp.repeat(jnp.exp(draws), shape[axis_at] // blocks).reshape((-1,) + (1,) * (len(shape) - 1 - axis_at))
    return factor_of


def profile(count, total, limit, lean):
    portions = [(1 << 20) // math.isqrt(grade ** lean) + 1 for grade in range(2, count + 1)]
    spare, holding = total - limit - (count - 1), [1] * (count - 1)
    while spare > 0:
        movable = [i for i in range(count - 1) if holding[i] < limit]
        mass, left = sum([portions[i] for i in movable]), spare
        for i in movable:
            more = min(limit - holding[i], max(1, left * portions[i] // mass), spare)
            holding[i] = holding[i] + more
            spare = spare - more
    return np.array([limit] + holding)


def uneven_parts(stream_key, number_of, total, reach, skew):
    if number_of == 2:
        one = jax.random.randint(stream_key, (), max(1, total - reach), min(reach, total - 1) + 1)
        return jnp.stack([one, total - one])
    lengths = jnp.asarray(profile(number_of, total, reach, skew), jnp.int32)
    twos = (number_of - 1) // 2
    source_of, sink = lengths[1:1 + 2 * twos:2], lengths[2:2 + 2 * twos:2]
    slack = jnp.minimum(source_of - 1, reach - sink)
    passed = jax.random.randint(jax.random.fold_in(stream_key, 1), (twos,), 0, 1 << 20) % (slack + 1)
    lengths = lengths.at[1:1 + 2 * twos:2].set(source_of - passed).at[2:2 + 2 * twos:2].set(sink + passed)
    return lengths[jax.random.permutation(jax.random.fold_in(stream_key, 2), number_of)]


def gaussian(rng, shape, spread, limit, split=(), held_as=jnp.bfloat16):
    drawn = spread * jax.random.normal(rng, shape, jnp.float32)
    if split:
        drawn = drawn * block_scale(rng, shape, split, -0.22, 0.18)
    return jnp.clip(drawn, -limit, limit).astype(held_as)


def setup_inputs(seed: int = 0) -> dict:
    key_list = jax.random.split(jax.random.key(seed), 7)
    return {
        "frames": gaussian(key_list[0], (FRAMES, TILE_H, TILE_W, C_IN), 1.0, 6.0, ((0, 32),)),
        "clip_blocks": uneven_parts(key_list[1], CLIPS, N_DP, MOST, 2).astype(jnp.int32),
        "tail_frames": set_ends(jax.random.randint(key_list[2], (CLIPS,), 1, GROUP + 1), jax.random.fold_in(key_list[2], 1), 1, GROUP).astype(jnp.int32),
        "weight_one": gaussian(key_list[3], (3, 3, 3, C_IN, C_MID), (27 * C_IN) ** -0.5, 0.109375),
        "weight_two": gaussian(key_list[4], (3, 3, 3, C_MID, C_OUT), (27 * C_MID) ** -0.5, 0.109375),
        "cotangent": gaussian(key_list[5], (FRAMES, TILE_H, TILE_W, C_OUT), 1.0, 6.0, ((0, 32),)),
    }


def conv_level(inp, weight):
    return lax.conv_general_dilated(inp, weight, (1, 1, 1), ((0, 0), (1, 1), (1, 1)), dimension_numbers=('NDHWC', 'DHWIO', 'NDHWC'), preferred_element_type=jnp.float32)

def conv_back(grad, weight):
    padded = jnp.pad(grad, ((0, 0), (2, 2), (0, 0), (0, 0), (0, 0)))
    flipped = jnp.swapaxes(jnp.flip(weight, (0, 1, 2)), 3, 4)
    return conv_level(padded, flipped)

def kernel_grad(extended, grad):
    count = grad.shape[-4]
    height = grad.shape[-3]
    width = grad.shape[-2]
    padded = jnp.pad(extended, ((0, 0), (0, 0), (1, 1), (1, 1), (0, 0)))
    rows = grad.reshape(-1, grad.shape[-1])
    taps = []
    for kt in range(3):
        for kh in range(3):
            for kw in range(3):
                window = padded[:, kt:kt + count, kh:kh + height, kw:kw + width, :]
                taps.append(jnp.dot(window.reshape(-1, window.shape[-1]).T, rows, preferred_element_type=jnp.float32))
    return jnp.stack(taps).reshape(3, 3, 3, extended.shape[-1], grad.shape[-1])

def silu_slope(value):
    sig = jax.nn.sigmoid(value)
    return sig * (1.0 + value * (1.0 - sig))

def reference(frames, clip_blocks, tail_frames, weight_one, weight_two, cotangent):
    blocks = N_DP
    ends = jnp.cumsum(clip_blocks).astype(jnp.int32)
    starts = ends - clip_blocks
    index = jnp.arange(blocks, dtype=jnp.int32)
    is_start = jnp.any(starts[None, :] == index[:, None], axis=1)
    keep = jnp.where(is_start, 0.0, 1.0).astype(jnp.bfloat16)
    last_match = ends[None, :] - 1 == index[:, None]
    is_last = jnp.any(last_match, axis=1)
    tail_here = lax.optimization_barrier(jnp.sum(jnp.where(last_match, tail_frames[None, :], 0), axis=1)).astype(jnp.int32)
    valid = jnp.where(is_last, tail_here, GROUP).astype(jnp.int32)
    used = jnp.arange(GROUP, dtype=jnp.int32)[None, :] < valid[:, None]
    used = used[:, :, None, None, None]
    xin = frames.reshape(blocks, GROUP, TILE_H, TILE_W, C_IN)
    prev_x = jnp.concatenate([jnp.zeros_like(xin[:1, :2]), xin[:-1, GROUP - 2:]], axis=0) * keep[:, None, None, None, None]
    xext = jnp.concatenate([prev_x, xin], axis=1)
    pre = conv_level(xext, weight_one)
    hidden = jax.nn.silu(pre).astype(jnp.bfloat16)
    prev_h = jnp.concatenate([jnp.zeros_like(hidden[:1, :2]), hidden[:-1, GROUP - 2:]], axis=0) * keep[:, None, None, None, None]
    hext = jnp.concatenate([prev_h, hidden], axis=1)
    out = conv_level(hext, weight_two)
    features = jnp.where(used, out, 0.0).astype(jnp.bfloat16)
    scale = 1.0 / jnp.sqrt(jnp.float32(FRAMES * TILE_H * TILE_W))
    cot = cotangent.reshape(blocks, GROUP, TILE_H, TILE_W, C_OUT).astype(jnp.float32)
    dout = (jnp.where(used, cot, 0.0) * scale).astype(jnp.bfloat16)
    grad_two = kernel_grad(hext, dout)
    back = conv_back(dout, weight_two)
    carried = back[:, :2] * keep.astype(jnp.float32)[:, None, None, None, None]
    carried = jnp.concatenate([carried[1:], jnp.zeros_like(carried[:1])], axis=0)
    dhid = back[:, 2:] + jnp.concatenate([jnp.zeros_like(back[:, :GROUP - 2]), carried], axis=1)
    dpre = (dhid * silu_slope(pre)).astype(jnp.bfloat16)
    grad_one = kernel_grad(xext, dpre)
    return (features.reshape(FRAMES, TILE_H, TILE_W, C_OUT), grad_one, grad_two)
```

```python
import functools
import math

import jax
import jax.numpy as jnp
from jax import lax
from jax.experimental import pallas as pl
from jax.experimental.pallas import tpu as pltpu
from jax.sharding import PartitionSpec as P

LANES = 128


def bit_order(chunk, levels):
    middle = list(range(1, levels - 1))
    turn = chunk % max(1, len(middle))
    return [0] + middle[turn:] + middle[:turn] + [levels - 1]


def sum_kernel(levels, one_ref, two_ref, out_ref, acc, sent, came, rs_send, rs_recv, ag_send, ag_recv):
    chunks, rows = (acc.shape[0], acc.shape[1])
    real = one_ref.shape[0]
    me = lax.axis_index("dp")
    bits = [lax.rem(me // (1 << k), 2) for k in range(levels)]
    partners = [me + (1 - 2 * bits[k]) * (1 << k) for k in range(levels)]
    orders = [bit_order(chunk, levels) for chunk in range(chunks)]

    barrier = pltpu.get_barrier_semaphore()
    for k in range(levels):
        pl.semaphore_signal(barrier, inc=1, device_id=(partners[k],), device_id_type=pl.DeviceIdType.MESH)

    wide = one_ref.shape[1] // LANES
    for chunk in range(chunks):
        ref, col = (one_ref, chunk) if chunk < wide else (two_ref, chunk - wide)
        acc[chunk, :real, :] = ref[:, col * LANES : (col + 1) * LANES]
        if rows > real:
            acc[chunk, real:, :] = jnp.zeros((rows - real, LANES), jnp.float32)

    pl.semaphore_wait(barrier, levels)

    def aligned(value):
        return pl.multiple_of(value, 16)

    def scatter_copy(chunk, step):
        size = rows >> (step + 1)
        at = rows - (rows >> step)
        return pltpu.make_async_remote_copy(
            src_ref=sent.at[chunk, pl.ds(at, size)],
            dst_ref=came.at[chunk, pl.ds(at, size)],
            send_sem=rs_send.at[chunk, step],
            recv_sem=rs_recv.at[chunk, step],
            device_id=(partners[orders[chunk][step]],),
            device_id_type=pl.DeviceIdType.MESH,
        )

    def gather_copy(chunk, step, base):
        size = rows >> (step + 1)
        return pltpu.make_async_remote_copy(
            src_ref=out_ref.at[chunk, pl.ds(aligned(base), size)],
            dst_ref=out_ref.at[chunk, pl.ds(aligned(base), size)],
            send_sem=ag_send.at[chunk, step],
            recv_sem=ag_recv.at[chunk, step],
            device_id=(partners[orders[chunk][step]],),
            device_id_type=pl.DeviceIdType.MESH,
        )

    base = [jnp.int32(0)] * chunks
    copies = [None] * chunks
    pending = []

    def send_half(chunk, step):
        size = rows >> (step + 1)
        at = rows - (rows >> step)
        bit = bits[orders[chunk][step]]
        away = aligned(base[chunk] + (1 - bit) * size)
        sent[chunk, pl.ds(at, size), :] = acc[chunk, pl.ds(away, size), :].astype(jnp.bfloat16)
        copies[chunk] = scatter_copy(chunk, step)
        copies[chunk].start()
        pending.append(copies[chunk])
        base[chunk] = base[chunk] + bit * size

    for chunk in range(chunks):
        send_half(chunk, 0)
    for step in range(levels):
        size = rows >> (step + 1)
        at = rows - (rows >> step)
        for chunk in range(chunks):
            copies[chunk].wait_recv()
            here = pl.ds(aligned(base[chunk]), size)
            total = acc[chunk, here, :] + came[chunk, pl.ds(at, size), :].astype(jnp.float32)
            if step + 1 < levels:
                acc[chunk, here, :] = total
                send_half(chunk, step + 1)
            else:
                out_ref[chunk, here, :] = total.astype(jnp.bfloat16)
                copies[chunk] = gather_copy(chunk, step, base[chunk])
                copies[chunk].start()
                pending.append(copies[chunk])
    for step in reversed(range(levels)):
        size = rows >> (step + 1)
        for chunk in range(chunks):
            copies[chunk].wait_recv()
            base[chunk] = base[chunk] - bits[orders[chunk][step]] * size
            if step > 0:
                copies[chunk] = gather_copy(chunk, step - 1, base[chunk])
                copies[chunk].start()
                pending.append(copies[chunk])
    for copy in pending:
        copy.wait_send()


def sum_over_devices(one, two):
    devices = lax.axis_size("dp")
    levels = devices.bit_length() - 1
    assert devices == 1 << levels
    shape_one, shape_two = (one.shape, two.shape)
    one = one.reshape(-1, one.shape[-1])
    two = two.reshape(-1, two.shape[-1])
    real = one.shape[0]
    step = 16 * devices
    rows = -(-real // step) * step
    chunks = (one.shape[1] + two.shape[1]) // LANES
    summed = pl.pallas_call(
        functools.partial(sum_kernel, levels),
        out_shape=jax.ShapeDtypeStruct((chunks, rows, LANES), jnp.bfloat16),
        in_specs=[pl.BlockSpec(memory_space=pltpu.VMEM)] * 2,
        out_specs=pl.BlockSpec(memory_space=pltpu.VMEM),
        scratch_shapes=[
            pltpu.VMEM((chunks, rows, LANES), jnp.float32),
            pltpu.VMEM((chunks, rows, LANES), jnp.bfloat16),
            pltpu.VMEM((chunks, rows, LANES), jnp.bfloat16),
        ]
        + [pltpu.SemaphoreType.DMA((chunks, levels))] * 4,
        compiler_params=pltpu.CompilerParams(
            collective_id=0, has_side_effects=True, vmem_limit_bytes=40 * 1024 * 1024
        ),
    )(one, two)
    summed = summed[:, :real].astype(jnp.float32)
    wide = one.shape[1] // LANES
    whole = [summed[chunk] for chunk in range(chunks)]
    grad_one = jnp.concatenate(whole[:wide], axis=1).reshape(shape_one)
    grad_two = jnp.concatenate(whole[wide:], axis=1).reshape(shape_two)
    return grad_one, grad_two


def from_behind(value, axis, steps):
    count = lax.axis_size(axis)
    initial, last = (max(0, -steps), min(count, count - steps))
    return lax.ppermute(value, axis, [(source, source + steps) for source in range(initial, last)])


def conv_level(inp, weight):
    return lax.conv_general_dilated(
        inp[None],
        weight,
        (1, 1, 1),
        ((0, 0), (1, 1), (1, 1)),
        dimension_numbers=("NDHWC", "DHWIO", "NDHWC"),
        preferred_element_type=jnp.float32,
    )[0]


def conv_back(grad, weight):
    padded = jnp.pad(grad, ((2, 2), (0, 0), (0, 0), (0, 0)))
    flipped = jnp.swapaxes(jnp.flip(weight, (0, 1, 2)), 3, 4)
    return conv_level(padded, flipped)


def kernel_grad(extended, grad):
    count = grad.shape[0]
    height = grad.shape[1]
    width = grad.shape[2]
    padded = jnp.pad(extended, ((0, 0), (1, 1), (1, 1), (0, 0)))
    rows = grad.reshape(-1, grad.shape[-1])
    taps = []
    for kt in range(3):
        for kh in range(3):
            for kw in range(3):
                window = padded[kt : kt + count, kh : kh + height, kw : kw + width, :]
                taps.append(
                    jnp.dot(
                        window.reshape(-1, window.shape[-1]).T,
                        rows,
                        preferred_element_type=jnp.float32,
                    )
                )
    return jnp.stack(taps).reshape(3, 3, 3, extended.shape[-1], grad.shape[-1])


def silu_slope(value):
    sig = jax.nn.sigmoid(value)
    return sig * (1.0 + value * (1.0 - sig))


def local(frames, clip_blocks, tail_frames, weight_one, weight_two, cotangent):
    count = frames.shape[0]
    devices = lax.axis_size("dp")
    place = lax.axis_index("dp")
    ends = jnp.cumsum(clip_blocks)
    starts = ends - clip_blocks
    is_start = jnp.any(starts == place)
    keep = jnp.where(is_start, 0.0, 1.0)
    last_match = ends - 1 == place
    tail_here = jnp.sum(jnp.where(last_match, tail_frames, 0))
    valid = jnp.where(jnp.any(last_match), tail_here, count)
    used = (jnp.arange(count, dtype=jnp.int32) < valid)[:, None, None, None]
    keep_low = keep.astype(jnp.bfloat16)
    arrived = from_behind(frames[count - 4 :], "dp", 1) * keep_low
    xext = jnp.concatenate([arrived[2:], frames], axis=0)
    pre = conv_level(xext, weight_one)
    hidden = jax.nn.silu(pre).astype(jnp.bfloat16)
    prev_h = jax.nn.silu(conv_level(arrived, weight_one)).astype(jnp.bfloat16) * keep_low
    hext = jnp.concatenate([prev_h, hidden], axis=0)
    out = conv_level(hext, weight_two)
    features = jnp.where(used, out, 0.0).astype(jnp.bfloat16)
    scale = 1.0 / math.sqrt(devices * count * frames.shape[1] * frames.shape[2])
    dout = (jnp.where(used, cotangent.astype(jnp.float32), 0.0) * scale).astype(jnp.bfloat16)
    local_two = kernel_grad(hext, dout)
    back = conv_back(dout, weight_two)
    carried = from_behind((back[:2] * keep).astype(jnp.bfloat16), "dp", -1).astype(jnp.float32)
    dhid = back[2:] + jnp.concatenate([jnp.zeros_like(back[: count - 2]), carried], axis=0)
    dpre = (dhid * silu_slope(pre)).astype(jnp.bfloat16)
    local_one = kernel_grad(xext, dpre)
    grad_one, grad_two = sum_over_devices(local_one, local_two)
    return (features, grad_one, grad_two)


def solution(mesh):
    return jax.shard_map(
        local,
        mesh=mesh,
        in_specs=(P("dp", None, None, None), P(), P(), P(), P(), P("dp", None, None, None)),
        out_specs=(P("dp", None, None, None), P(), P()),
        check_vma=False,
    )
```

```python
import functools
import math

import jax
import jax.numpy as jnp
from jax import lax
from jax.experimental import pallas as pl
from jax.experimental.pallas import tpu as pltpu
from jax.sharding import PartitionSpec as P

LANES = 128


def bit_order(chunk, levels):
    middle = list(range(1, levels - 1))
    turn = chunk % max(1, len(middle))
    return [0] + middle[turn:] + middle[:turn] + [levels - 1]


def sum_kernel(levels, one_ref, two_ref, out_ref, acc, sent, came, rs_send, rs_recv, ag_send, ag_recv):
    chunks, rows = (acc.shape[0], acc.shape[1])
    real = one_ref.shape[0]
    me = lax.axis_index("dp")
    bits = [lax.rem(me // (1 << k), 2) for k in range(levels)]
    partners = [me + (1 - 2 * bits[k]) * (1 << k) for k in range(levels)]
    orders = [bit_order(chunk, levels) for chunk in range(chunks)]

    barrier = pltpu.get_barrier_semaphore()
    for k in range(levels):
        pl.semaphore_signal(barrier, inc=1, device_id=(partners[k],), device_id_type=pl.DeviceIdType.MESH)

    wide = one_ref.shape[1] // LANES
    for chunk in range(chunks):
        ref, col = (one_ref, chunk) if chunk < wide else (two_ref, chunk - wide)
        acc[chunk, :real, :] = ref[:, col * LANES : (col + 1) * LANES]
        if rows > real:
            acc[chunk, real:, :] = jnp.zeros((rows - real, LANES), jnp.float32)

    pl.semaphore_wait(barrier, levels)

    def aligned(value):
        return pl.multiple_of(value, 16)

    def scatter_copy(chunk, step):
        size = rows >> (step + 1)
        at = rows - (rows >> step)
        return pltpu.make_async_remote_copy(
            src_ref=sent.at[chunk, pl.ds(at, size)],
            dst_ref=came.at[chunk, pl.ds(at, size)],
            send_sem=rs_send.at[chunk, step],
            recv_sem=rs_recv.at[chunk, step],
            device_id=(partners[orders[chunk][step]],),
            device_id_type=pl.DeviceIdType.MESH,
        )

    def gather_copy(chunk, step, base):
        size = rows >> (step + 1)
        return pltpu.make_async_remote_copy(
            src_ref=out_ref.at[chunk, pl.ds(aligned(base), size)],
            dst_ref=out_ref.at[chunk, pl.ds(aligned(base), size)],
            send_sem=ag_send.at[chunk, step],
            recv_sem=ag_recv.at[chunk, step],
            device_id=(partners[orders[chunk][step]],),
            device_id_type=pl.DeviceIdType.MESH,
        )

    base = [jnp.int32(0)] * chunks
    copies = [None] * chunks
    pending = []

    def send_half(chunk, step):
        size = rows >> (step + 1)
        at = rows - (rows >> step)
        bit = bits[orders[chunk][step]]
        away = aligned(base[chunk] + (1 - bit) * size)
        sent[chunk, pl.ds(at, size), :] = acc[chunk, pl.ds(away, size), :].astype(jnp.bfloat16)
        copies[chunk] = scatter_copy(chunk, step)
        copies[chunk].start()
        pending.append(copies[chunk])
        base[chunk] = base[chunk] + bit * size

    for chunk in range(chunks):
        send_half(chunk, 0)
    for step in range(levels):
        size = rows >> (step + 1)
        at = rows - (rows >> step)
        for chunk in range(chunks):
            copies[chunk].wait_recv()
            here = pl.ds(aligned(base[chunk]), size)
            total = acc[chunk, here, :] + came[chunk, pl.ds(at, size), :].astype(jnp.float32)
            if step + 1 < levels:
                acc[chunk, here, :] = total
                send_half(chunk, step + 1)
            else:
                out_ref[chunk, here, :] = total.astype(jnp.bfloat16)
                copies[chunk] = gather_copy(chunk, step, base[chunk])
                copies[chunk].start()
                pending.append(copies[chunk])
    for step in reversed(range(levels)):
        size = rows >> (step + 1)
        for chunk in range(chunks):
            copies[chunk].wait_recv()
            base[chunk] = base[chunk] - bits[orders[chunk][step]] * size
            if step > 0:
                copies[chunk] = gather_copy(chunk, step - 1, base[chunk])
                copies[chunk].start()
                pending.append(copies[chunk])
    for copy in pending:
        copy.wait_send()


def sum_over_devices(one, two):
    devices = lax.axis_size("dp")
    levels = devices.bit_length() - 1
    assert devices == 1 << levels
    shape_one, shape_two = (one.shape, two.shape)
    one = one.reshape(-1, one.shape[-1])
    two = two.reshape(-1, two.shape[-1])
    real = one.shape[0]
    step = 16 * devices
    rows = -(-real // step) * step
    chunks = (one.shape[1] + two.shape[1]) // LANES
    summed = pl.pallas_call(
        functools.partial(sum_kernel, levels),
        out_shape=jax.ShapeDtypeStruct((chunks, rows, LANES), jnp.bfloat16),
        in_specs=[pl.BlockSpec(memory_space=pltpu.VMEM)] * 2,
        out_specs=pl.BlockSpec(memory_space=pltpu.VMEM),
        scratch_shapes=[
            pltpu.VMEM((chunks, rows, LANES), jnp.float32),
            pltpu.VMEM((chunks, rows, LANES), jnp.bfloat16),
            pltpu.VMEM((chunks, rows, LANES), jnp.bfloat16),
        ]
        + [pltpu.SemaphoreType.DMA((chunks, levels))] * 4,
        compiler_params=pltpu.CompilerParams(
            collective_id=0, has_side_effects=True, vmem_limit_bytes=40 * 1024 * 1024
        ),
    )(one, two)
    summed = summed[:, :real].astype(jnp.float32)
    wide = one.shape[1] // LANES
    whole = [summed[chunk] for chunk in range(chunks)]
    grad_one = jnp.concatenate(whole[:wide], axis=1).reshape(shape_one)
    grad_two = jnp.concatenate(whole[wide:], axis=1).reshape(shape_two)
    return grad_one, grad_two


def from_behind(value, axis, steps):
    count = lax.axis_size(axis)
    initial, last = (max(0, -steps), min(count, count - steps))
    return lax.ppermute(value, axis, [(source, source + steps) for source in range(initial, last)])


def spread(source, target, width):
    count, pixels, channels = source.shape
    column = lax.broadcasted_iota(jnp.int32, (pixels, channels), 0) % width

    @pl.loop(0, count)
    def _(f):
        value = source[f]
        wide = value.astype(jnp.float32)
        left = jnp.where(column == 0, 0.0, pltpu.roll(wide, 1, 0)).astype(jnp.bfloat16)
        right = jnp.where(column == width - 1, 0.0, pltpu.roll(wide, pixels - 1, 0)).astype(jnp.bfloat16)
        blank = jnp.zeros((width, channels), jnp.bfloat16)
        for kw, moved in enumerate((left, value, right)):
            target[f, :, (3 + kw) * channels : (4 + kw) * channels] = moved
            cols = slice(kw * channels, (kw + 1) * channels)
            target[f, width:, cols] = moved[: pixels - width]
            target[f, :width, cols] = blank
            cols = slice((6 + kw) * channels, (7 + kw) * channels)
            target[f, : pixels - width, cols] = moved[width:]
            target[f, pixels - width :, cols] = blank


def turn(taps, first, turned, channels):
    pixels = taps.shape[1]

    @pl.loop(0, turned.shape[1] // pixels)
    def _(f):
        at = pl.ds(pl.multiple_of(f * pixels, pixels), pixels)
        for tap in range(9):
            cols = slice(tap * channels, (tap + 1) * channels)
            turned[cols, at] = taps[first + f, :, cols].T


def outer(turned, grad, result, pixels):
    rows = grad.shape[0]
    height = turned.shape[0] // 3
    for kt in range(3):

        @pl.loop(0, 3)
        def _(kh):
            at = pl.ds(pl.multiple_of(kh * height, height), height)
            result[kt, at, :] = jnp.dot(
                turned[at, kt * pixels : kt * pixels + rows], grad[...], preferred_element_type=jnp.float32
            )


def back_kernel(width, scale, valid_ref, cot_ref, weight_ref, dout_ref, head_ref, tail_ref, taps, flipped, back):
    count, pixels, channels = cot_ref.shape
    inner = tail_ref.shape[2]
    valid = valid_ref[0]

    @pl.loop(0, count)
    def _(f):
        used = jnp.where(f < valid, jnp.float32(1.0), jnp.float32(0.0))
        dout_ref[f] = ((cot_ref[f].astype(jnp.float32) * used) * scale).astype(jnp.bfloat16)

    spread(dout_ref, taps, width)
    for kt in range(3):
        for tap in range(9):
            flipped[tap * channels : (tap + 1) * channels, kt * inner : (kt + 1) * inner] = weight_ref[kt, 8 - tap].T
    back[...] = jnp.zeros_like(back)

    @pl.loop(0, count // 2)
    def _(g):
        f = g * 2
        part = jnp.dot(
            taps[pl.ds(f, 2)].reshape(2 * pixels, 9 * channels), flipped[...], preferred_element_type=jnp.float32
        ).reshape(2, pixels, 3 * inner)
        for kt in range(3):
            back[pl.ds(f + kt, 2)] += part[:, :, kt * inner : (kt + 1) * inner]

    head_ref[...] = back[:2].astype(jnp.bfloat16)
    tail_ref[...] = back[2:]


def forward_kernel(
    width, scalars_ref, ext_ref, one_ref, two_ref, dout_ref, feat_ref, pre_ref, grad_ref, taps, turned, pre, hidden
):
    total, pixels, channels = ext_ref.shape
    count = total - 4
    inner = one_ref.shape[2]
    outer_channels = two_ref.shape[2]
    keep, valid = (scalars_ref[0], scalars_ref[1])
    spread(ext_ref, taps, width)
    pre[...] = jnp.zeros_like(pre)

    @pl.loop(0, total // 2)
    def _(g):
        f = g * 2
        weight = jnp.concatenate([one_ref[0], one_ref[1], one_ref[2]], axis=1)
        part = jnp.dot(
            taps[pl.ds(f, 2)].reshape(2 * pixels, 9 * channels), weight, preferred_element_type=jnp.float32
        ).reshape(2, pixels, 3 * inner)
        for kt in range(3):
            pre[pl.ds(f + 2 - kt, 2)] += part[:, :, kt * inner : (kt + 1) * inner]

    pre_ref[...] = pre[4 : 4 + count]

    @pl.loop(0, count + 2)
    def _(f):
        value = pre[f + 2]
        held = jnp.where((f >= 2) | (keep > 0), jnp.float32(1.0), jnp.float32(0.0))
        hidden[f] = (jax.nn.silu(value) * held).astype(jnp.bfloat16)

    spread(hidden, taps, width)

    @pl.loop(0, count // 2)
    def _(g):
        f = g * 2
        total_out = jnp.zeros((2 * pixels, outer_channels), jnp.float32)
        for kt in range(3):
            total_out += jnp.dot(
                taps[pl.ds(f + kt, 2)].reshape(2 * pixels, 9 * inner), two_ref[kt], preferred_element_type=jnp.float32
            )
        total_out = total_out.reshape(2, pixels, outer_channels)
        for i in range(2):
            used = jnp.broadcast_to(f + i < valid, (pixels, outer_channels))
            feat_ref[f + i] = jnp.where(used, total_out[i], 0.0).astype(jnp.bfloat16)

    turn(taps, 0, turned, inner)
    outer(turned, dout_ref, grad_ref, pixels)


def last_kernel(width, ext_ref, pre_ref, tail_ref, carried_ref, grad_ref, taps, turned, dpre):
    count, pixels, inner = pre_ref.shape
    channels = ext_ref.shape[2]
    spread(ext_ref.at[pl.ds(2, count + 2)], taps, width)
    turn(taps, 0, turned, channels)

    @pl.loop(0, count)
    def _(f):
        dhid = tail_ref[f]
        more = carried_ref[jnp.maximum(f - (count - 2), 0)].astype(jnp.float32)
        dhid = dhid + jnp.where(jnp.broadcast_to(f >= count - 2, more.shape), more, 0.0)
        at = pl.ds(pl.multiple_of(f * pixels, pixels), pixels)
        dpre[at, :] = (dhid * silu_slope(pre_ref[f])).astype(jnp.bfloat16)

    outer(turned, dpre, grad_ref, pixels)


def silu_slope(value):
    sig = jax.nn.sigmoid(value)
    return sig * (1.0 + value * (1.0 - sig))


VMEM = pl.BlockSpec(memory_space=pltpu.VMEM)
SMEM = pl.BlockSpec(memory_space=pltpu.SMEM)
PARAMS = pltpu.CompilerParams(vmem_limit_bytes=56 * 1024 * 1024)


def local(frames, clip_blocks, tail_frames, weight_one, weight_two, cotangent):
    count, height, width, channels = frames.shape
    pixels = height * width
    inner = weight_one.shape[-1]
    wide = weight_two.shape[-1]
    bf16, f32 = (jnp.bfloat16, jnp.float32)
    devices = lax.axis_size("dp")
    place = lax.axis_index("dp")
    frames = frames.reshape(count, pixels, channels)
    cotangent = cotangent.reshape(count, pixels, wide)
    one = weight_one.reshape(3, 9 * channels, inner)
    arrived = from_behind(frames[count - 4 :], "dp", 1)
    order = jnp.arange(clip_blocks.shape[0])
    ends = jnp.sum(jnp.where(order[None, :] <= order[:, None], clip_blocks[None, :], 0), axis=1)
    keep = jnp.where(jnp.any(ends - clip_blocks == place), 0, 1).astype(jnp.int32)
    last_match = ends - 1 == place
    tail_here = jnp.sum(jnp.where(last_match, tail_frames, 0))
    valid = jnp.where(jnp.any(last_match), tail_here, count).astype(jnp.int32)
    scalars = jnp.stack([keep, valid])
    scale = 1.0 / math.sqrt(devices * count * pixels)

    dout, head, tail = pl.pallas_call(
        functools.partial(back_kernel, width, scale),
        out_shape=(
            jax.ShapeDtypeStruct((count, pixels, wide), bf16),
            jax.ShapeDtypeStruct((2, pixels, inner), bf16),
            jax.ShapeDtypeStruct((count, pixels, inner), f32),
        ),
        in_specs=[SMEM, VMEM, VMEM],
        out_specs=(VMEM, VMEM, VMEM),
        scratch_shapes=[
            pltpu.VMEM((count, pixels, 9 * wide), bf16),
            pltpu.VMEM((9 * wide, 3 * inner), bf16),
            pltpu.VMEM((count + 2, pixels, inner), f32),
        ],
        compiler_params=PARAMS,
        cost_estimate=pl.CostEstimate(flops=10**10, bytes_accessed=5 * 10**6, transcendentals=0),
    )(scalars[1:], cotangent, weight_two.reshape(3, 9, inner, wide))
    carried = from_behind(head * keep.astype(bf16), "dp", -1)
    ext = jnp.concatenate([arrived * keep.astype(bf16), frames], axis=0)
    features, pre, grad_two = pl.pallas_call(
        functools.partial(forward_kernel, width),
        out_shape=(
            jax.ShapeDtypeStruct((count, pixels, wide), bf16),
            jax.ShapeDtypeStruct((count, pixels, inner), f32),
            jax.ShapeDtypeStruct((3, 9 * inner, wide), f32),
        ),
        in_specs=[SMEM, VMEM, VMEM, VMEM, VMEM],
        out_specs=(VMEM, VMEM, VMEM),
        scratch_shapes=[
            pltpu.VMEM((count + 4, pixels, 9 * max(channels, inner)), bf16),
            pltpu.VMEM((9 * inner, (count + 2) * pixels), bf16),
            pltpu.VMEM((count + 6, pixels, inner), f32),
            pltpu.VMEM((count + 2, pixels, inner), bf16),
        ],
        compiler_params=PARAMS,
        cost_estimate=pl.CostEstimate(flops=12 * 10**9, bytes_accessed=12 * 10**6, transcendentals=0),
    )(scalars, ext, one, weight_two.reshape(3, 9 * inner, wide), dout.reshape(count * pixels, wide))
    grad_one = pl.pallas_call(
        functools.partial(last_kernel, width),
        out_shape=jax.ShapeDtypeStruct((3, 9 * channels, inner), f32),
        in_specs=[VMEM] * 4,
        out_specs=VMEM,
        scratch_shapes=[
            pltpu.VMEM((count + 2, pixels, 9 * channels), bf16),
            pltpu.VMEM((9 * channels, (count + 2) * pixels), bf16),
            pltpu.VMEM((count * pixels, inner), bf16),
        ],
        compiler_params=PARAMS,
        cost_estimate=pl.CostEstimate(flops=4 * 10**9, bytes_accessed=5 * 10**6, transcendentals=0),
    )(ext, pre, tail, carried)
    grad_one, grad_two = sum_over_devices(grad_one, grad_two)
    return (
        features.reshape(count, height, width, wide),
        grad_one.reshape(weight_one.shape),
        grad_two.reshape(weight_two.shape),
    )


def solution(mesh):
    return jax.shard_map(
        local,
        mesh=mesh,
        in_specs=(P("dp", None, None, None), P(), P(), P(), P(), P("dp", None, None, None)),
        out_specs=(P("dp", None, None, None), P(), P()),
        check_vma=False,
    )
```

```python
import functools
import math

import jax
import jax.numpy as jnp
from jax import lax
from jax.experimental import pallas as pl
from jax.experimental.pallas import tpu as pltpu
from jax.sharding import PartitionSpec as P

LANES = 128


def bit_order(chunk, levels):
    middle = list(range(1, levels - 1))
    turn = chunk % max(1, len(middle))
    return [0] + middle[turn:] + middle[:turn] + [levels - 1]


def sum_kernel(
    levels,
    width,
    ext_ref,
    pre_ref,
    tail_ref,
    carried_ref,
    two_ref,
    out_one,
    out_two,
    acc,
    sent,
    came,
    taps,
    turned,
    dpre,
    rs_send,
    rs_recv,
    ag_send,
    ag_recv,
):
    chunks, rows = (acc.shape[0], acc.shape[1])
    count, pixels, inner = pre_ref.shape
    channels = ext_ref.shape[2]
    real = two_ref.shape[0]
    me = lax.axis_index("dp")
    bits = [lax.rem(me // (1 << k), 2) for k in range(levels)]
    partners = [me + (1 - 2 * bits[k]) * (1 << k) for k in range(levels)]
    orders = [bit_order(chunk, levels) for chunk in range(chunks)]

    barrier = pltpu.get_barrier_semaphore()
    for k in range(levels):
        pl.semaphore_signal(barrier, inc=1, device_id=(partners[k],), device_id_type=pl.DeviceIdType.MESH)

    for chunk in range(chunks):
        if chunk:
            acc[chunk, :real, :] = two_ref[:, (chunk - 1) * LANES : chunk * LANES]
        if rows > real:
            acc[chunk, real:, :] = jnp.zeros((rows - real, LANES), jnp.float32)

    pl.semaphore_wait(barrier, levels)

    def aligned(value):
        return pl.multiple_of(value, 16)

    def landing(chunk, base, size):
        at = pl.ds(aligned(base), size)
        if chunk == 0:
            return out_one.at[at, :]
        return out_two.at[at, (chunk - 1) * LANES : chunk * LANES]

    def scatter_copy(chunk, step):
        size = rows >> (step + 1)
        at = rows - (rows >> step)
        return pltpu.make_async_remote_copy(
            src_ref=sent.at[chunk, pl.ds(at, size)],
            dst_ref=came.at[chunk, pl.ds(at, size)],
            send_sem=rs_send.at[chunk, step],
            recv_sem=rs_recv.at[chunk, step],
            device_id=(partners[orders[chunk][step]],),
            device_id_type=pl.DeviceIdType.MESH,
        )

    def gather_copy(chunk, step, base):
        size = rows >> (step + 1)
        return pltpu.make_async_remote_copy(
            src_ref=landing(chunk, base, size),
            dst_ref=landing(chunk, base, size),
            send_sem=ag_send.at[chunk, step],
            recv_sem=ag_recv.at[chunk, step],
            device_id=(partners[orders[chunk][step]],),
            device_id_type=pl.DeviceIdType.MESH,
        )

    base = [jnp.int32(0)] * chunks
    copies = [None] * chunks
    pending = []

    def start(chunk, copy):
        copies[chunk] = copy
        copy.start()
        pending.append(copy)

    def send_half(chunk, step):
        size = rows >> (step + 1)
        at = rows - (rows >> step)
        bit = bits[orders[chunk][step]]
        away = aligned(base[chunk] + (1 - bit) * size)
        sent[chunk, pl.ds(at, size), :] = acc[chunk, pl.ds(away, size), :].astype(jnp.bfloat16)
        start(chunk, scatter_copy(chunk, step))
        base[chunk] = base[chunk] + bit * size

    def scatter_step(chunk, step):
        size = rows >> (step + 1)
        at = rows - (rows >> step)
        copies[chunk].wait_recv()
        here = pl.ds(aligned(base[chunk]), size)
        total = acc[chunk, here, :] + came[chunk, pl.ds(at, size), :].astype(jnp.float32)
        if step + 1 < levels:
            acc[chunk, here, :] = total
            send_half(chunk, step + 1)
        else:
            landing(chunk, base[chunk], size)[...] = total.astype(jnp.bfloat16)
            start(chunk, gather_copy(chunk, step, base[chunk]))

    def gather_step(chunk, step):
        size = rows >> (step + 1)
        copies[chunk].wait_recv()
        base[chunk] = base[chunk] - bits[orders[chunk][step]] * size
        if step > 0:
            start(chunk, gather_copy(chunk, step - 1, base[chunk]))

    def steps(chunk):
        work = [functools.partial(send_half, chunk, 0)]
        work += [functools.partial(scatter_step, chunk, step) for step in range(levels)]
        return work + [functools.partial(gather_step, chunk, step) for step in reversed(range(levels))]

    def slope_part():
        @pl.loop(0, count)
        def _(f):
            dhid = tail_ref[f]
            more = carried_ref[jnp.maximum(f - (count - 2), 0)].astype(jnp.float32)
            dhid = dhid + jnp.where(jnp.broadcast_to(f >= count - 2, more.shape), more, 0.0)
            at = pl.ds(pl.multiple_of(f * pixels, pixels), pixels)
            dpre[at, :] = (dhid * silu_slope(pre_ref[f])).astype(jnp.bfloat16)

    def outer_part(kt):
        height = turned.shape[0] // 3

        @pl.loop(0, 3)
        def _(kh):
            at = pl.ds(pl.multiple_of(kh * height, height), height)
            into = pl.ds(pl.multiple_of((kt * 3 + kh) * height, height), height)
            acc[0, into, :] = jnp.dot(
                turned[at, kt * pixels : kt * pixels + count * pixels], dpre[...], preferred_element_type=jnp.float32
            )

    local = [
        functools.partial(spread, ext_ref.at[pl.ds(2, count + 2)], taps, width),
        functools.partial(turn, taps, 0, turned, channels),
        slope_part,
    ] + [functools.partial(outer_part, kt) for kt in range(3)]
    queues = [steps(chunk) for chunk in range(chunks)]
    for part in local:
        for chunk in range(1, chunks):
            if queues[chunk]:
                queues[chunk].pop(0)()
        part()
    while any(queues):
        for chunk in range(chunks):
            if queues[chunk]:
                queues[chunk].pop(0)()
    for copy in pending:
        copy.wait_send()


def sum_over_devices(width, ext, pre, tail, carried, two):
    devices = lax.axis_size("dp")
    levels = devices.bit_length() - 1
    assert devices == 1 << levels
    count, pixels, inner = pre.shape
    channels = ext.shape[2]
    assert inner == LANES
    two = two.reshape(-1, two.shape[-1])
    real, wide = two.shape
    step = 16 * devices
    rows = -(-real // step) * step
    chunks = 1 + wide // LANES
    one, two = pl.pallas_call(
        functools.partial(sum_kernel, levels, width),
        out_shape=(
            jax.ShapeDtypeStruct((rows, LANES), jnp.bfloat16),
            jax.ShapeDtypeStruct((rows, wide), jnp.bfloat16),
        ),
        in_specs=[pl.BlockSpec(memory_space=pltpu.VMEM)] * 5,
        out_specs=(pl.BlockSpec(memory_space=pltpu.VMEM),) * 2,
        scratch_shapes=[
            pltpu.VMEM((chunks, rows, LANES), jnp.float32),
            pltpu.VMEM((chunks, rows, LANES), jnp.bfloat16),
            pltpu.VMEM((chunks, rows, LANES), jnp.bfloat16),
            pltpu.VMEM((count + 2, pixels, 9 * channels), jnp.bfloat16),
            pltpu.VMEM((9 * channels, (count + 2) * pixels), jnp.bfloat16),
            pltpu.VMEM((count * pixels, inner), jnp.bfloat16),
        ]
        + [pltpu.SemaphoreType.DMA((chunks, levels))] * 4,
        compiler_params=pltpu.CompilerParams(
            collective_id=0, has_side_effects=True, vmem_limit_bytes=56 * 1024 * 1024
        ),
    )(ext, pre, tail, carried, two)
    return one[:real].astype(jnp.float32), two[:real].astype(jnp.float32)


def from_behind(value, axis, steps):
    count = lax.axis_size(axis)
    initial, last = (max(0, -steps), min(count, count - steps))
    return lax.ppermute(value, axis, [(source, source + steps) for source in range(initial, last)])


def spread(source, target, width):
    count, pixels, channels = source.shape
    column = lax.broadcasted_iota(jnp.int32, (pixels, channels), 0) % width

    @pl.loop(0, count)
    def _(f):
        value = source[f]
        wide = value.astype(jnp.float32)
        left = jnp.where(column == 0, 0.0, pltpu.roll(wide, 1, 0)).astype(jnp.bfloat16)
        right = jnp.where(column == width - 1, 0.0, pltpu.roll(wide, pixels - 1, 0)).astype(jnp.bfloat16)
        blank = jnp.zeros((width, channels), jnp.bfloat16)
        for kw, moved in enumerate((left, value, right)):
            target[f, :, (3 + kw) * channels : (4 + kw) * channels] = moved
            cols = slice(kw * channels, (kw + 1) * channels)
            target[f, width:, cols] = moved[: pixels - width]
            target[f, :width, cols] = blank
            cols = slice((6 + kw) * channels, (7 + kw) * channels)
            target[f, : pixels - width, cols] = moved[width:]
            target[f, pixels - width :, cols] = blank


def turn(taps, first, turned, channels):
    pixels = taps.shape[1]

    @pl.loop(0, turned.shape[1] // pixels)
    def _(f):
        at = pl.ds(pl.multiple_of(f * pixels, pixels), pixels)
        for tap in range(9):
            cols = slice(tap * channels, (tap + 1) * channels)
            turned[cols, at] = taps[first + f, :, cols].T


def outer(turned, grad, result, pixels):
    rows = grad.shape[0]
    height = turned.shape[0] // 3
    for kt in range(3):

        @pl.loop(0, 3)
        def _(kh):
            at = pl.ds(pl.multiple_of(kh * height, height), height)
            result[kt, at, :] = jnp.dot(
                turned[at, kt * pixels : kt * pixels + rows], grad[...], preferred_element_type=jnp.float32
            )


def clip_place(blocks_ref, tails_ref, count):
    place = lax.axis_index("dp")
    start, keep, valid = (jnp.int32(0), jnp.int32(1), jnp.int32(count))
    for clip in range(blocks_ref.shape[0]):
        keep = jnp.where(start == place, 0, keep)
        start = start + blocks_ref[clip]
        valid = jnp.where(start - 1 == place, tails_ref[clip], valid)
    return keep, valid


def back_kernel(width, scale, blocks_ref, tails_ref, cot_ref, weight_ref, dout_ref, head_ref, tail_ref, taps, flipped, back):
    count, pixels, channels = cot_ref.shape
    inner = tail_ref.shape[2]
    keep, valid = clip_place(blocks_ref, tails_ref, count)

    @pl.loop(0, count)
    def _(f):
        used = jnp.where(f < valid, jnp.float32(1.0), jnp.float32(0.0))
        dout_ref[f] = ((cot_ref[f].astype(jnp.float32) * used) * scale).astype(jnp.bfloat16)

    spread(dout_ref, taps, width)
    for kt in range(3):
        for tap in range(9):
            flipped[tap * channels : (tap + 1) * channels, kt * inner : (kt + 1) * inner] = weight_ref[kt, 8 - tap].T
    back[...] = jnp.zeros_like(back)

    @pl.loop(0, count // 2)
    def _(g):
        f = g * 2
        part = jnp.dot(
            taps[pl.ds(f, 2)].reshape(2 * pixels, 9 * channels), flipped[...], preferred_element_type=jnp.float32
        ).reshape(2, pixels, 3 * inner)
        for kt in range(3):
            back[pl.ds(f + kt, 2)] += part[:, :, kt * inner : (kt + 1) * inner]

    held = jnp.where(keep > 0, jnp.float32(1.0), jnp.float32(0.0))
    head_ref[...] = (back[:2] * held).astype(jnp.bfloat16)
    tail_ref[...] = back[2:]


def forward_kernel(
    width,
    blocks_ref,
    tails_ref,
    arrived_ref,
    frames_ref,
    one_ref,
    two_ref,
    dout_ref,
    feat_ref,
    pre_ref,
    grad_ref,
    ext_ref,
    taps,
    turned,
    pre,
    hidden,
):
    total, pixels, channels = ext_ref.shape
    count = total - 4
    inner = one_ref.shape[2]
    outer_channels = two_ref.shape[2]
    keep, valid = clip_place(blocks_ref, tails_ref, count)
    arrived = arrived_ref[...].astype(jnp.float32) * jnp.where(keep > 0, jnp.float32(1.0), jnp.float32(0.0))
    ext_ref[:4] = arrived.astype(jnp.bfloat16)
    ext_ref[4:] = frames_ref[...]
    spread(ext_ref, taps, width)
    pre[...] = jnp.zeros_like(pre)

    @pl.loop(0, total // 2)
    def _(g):
        f = g * 2
        weight = jnp.concatenate([one_ref[0], one_ref[1], one_ref[2]], axis=1)
        part = jnp.dot(
            taps[pl.ds(f, 2)].reshape(2 * pixels, 9 * channels), weight, preferred_element_type=jnp.float32
        ).reshape(2, pixels, 3 * inner)
        for kt in range(3):
            pre[pl.ds(f + 2 - kt, 2)] += part[:, :, kt * inner : (kt + 1) * inner]

    pre_ref[...] = pre[4 : 4 + count]

    @pl.loop(0, count + 2)
    def _(f):
        value = pre[f + 2]
        held = jnp.where((f >= 2) | (keep > 0), jnp.float32(1.0), jnp.float32(0.0))
        hidden[f] = (jax.nn.silu(value) * held).astype(jnp.bfloat16)

    spread(hidden, taps, width)

    @pl.loop(0, count // 2)
    def _(g):
        f = g * 2
        total_out = jnp.zeros((2 * pixels, outer_channels), jnp.float32)
        for kt in range(3):
            total_out += jnp.dot(
                taps[pl.ds(f + kt, 2)].reshape(2 * pixels, 9 * inner), two_ref[kt], preferred_element_type=jnp.float32
            )
        total_out = total_out.reshape(2, pixels, outer_channels)
        for i in range(2):
            used = jnp.broadcast_to(f + i < valid, (pixels, outer_channels))
            feat_ref[f + i] = jnp.where(used, total_out[i], 0.0).astype(jnp.bfloat16)

    turn(taps, 0, turned, inner)
    outer(turned, dout_ref, grad_ref, pixels)


def silu_slope(value):
    sig = jax.nn.sigmoid(value)
    return sig * (1.0 + value * (1.0 - sig))


VMEM = pl.BlockSpec(memory_space=pltpu.VMEM)
SMEM = pl.BlockSpec(memory_space=pltpu.SMEM)
PARAMS = pltpu.CompilerParams(vmem_limit_bytes=56 * 1024 * 1024)


def local(frames, clip_blocks, tail_frames, weight_one, weight_two, cotangent):
    count, height, width, channels = frames.shape
    pixels = height * width
    inner = weight_one.shape[-1]
    wide = weight_two.shape[-1]
    bf16, f32 = (jnp.bfloat16, jnp.float32)
    devices = lax.axis_size("dp")
    frames = frames.reshape(count, pixels, channels)
    cotangent = cotangent.reshape(count, pixels, wide)
    one = weight_one.reshape(3, 9 * channels, inner)
    arrived = from_behind(frames[count - 4 :], "dp", 1)
    scale = 1.0 / math.sqrt(devices * count * pixels)

    dout, head, tail = pl.pallas_call(
        functools.partial(back_kernel, width, scale),
        out_shape=(
            jax.ShapeDtypeStruct((count, pixels, wide), bf16),
            jax.ShapeDtypeStruct((2, pixels, inner), bf16),
            jax.ShapeDtypeStruct((count, pixels, inner), f32),
        ),
        in_specs=[SMEM, SMEM, VMEM, VMEM],
        out_specs=(VMEM, VMEM, VMEM),
        scratch_shapes=[
            pltpu.VMEM((count, pixels, 9 * wide), bf16),
            pltpu.VMEM((9 * wide, 3 * inner), bf16),
            pltpu.VMEM((count + 2, pixels, inner), f32),
        ],
        compiler_params=PARAMS,
        cost_estimate=pl.CostEstimate(flops=10**10, bytes_accessed=5 * 10**6, transcendentals=0),
    )(clip_blocks, tail_frames, cotangent, weight_two.reshape(3, 9, inner, wide))
    carried = from_behind(head, "dp", -1)
    features, pre, grad_two, ext = pl.pallas_call(
        functools.partial(forward_kernel, width),
        out_shape=(
            jax.ShapeDtypeStruct((count, pixels, wide), bf16),
            jax.ShapeDtypeStruct((count, pixels, inner), f32),
            jax.ShapeDtypeStruct((3, 9 * inner, wide), f32),
            jax.ShapeDtypeStruct((count + 4, pixels, channels), bf16),
        ),
        in_specs=[SMEM, SMEM, VMEM, VMEM, VMEM, VMEM, VMEM],
        out_specs=(VMEM, VMEM, VMEM, VMEM),
        scratch_shapes=[
            pltpu.VMEM((count + 4, pixels, 9 * max(channels, inner)), bf16),
            pltpu.VMEM((9 * inner, (count + 2) * pixels), bf16),
            pltpu.VMEM((count + 6, pixels, inner), f32),
            pltpu.VMEM((count + 2, pixels, inner), bf16),
        ],
        compiler_params=PARAMS,
        cost_estimate=pl.CostEstimate(flops=12 * 10**9, bytes_accessed=12 * 10**6, transcendentals=0),
    )(clip_blocks, tail_frames, arrived, frames, one, weight_two.reshape(3, 9 * inner, wide), dout.reshape(count * pixels, wide))
    grad_one, grad_two = sum_over_devices(width, ext, pre, tail, carried, grad_two)
    return (
        features.reshape(count, height, width, wide),
        grad_one.reshape(weight_one.shape),
        grad_two.reshape(weight_two.shape),
    )


def solution(mesh):
    return jax.shard_map(
        local,
        mesh=mesh,
        in_specs=(P("dp", None, None, None), P(), P(), P(), P(), P("dp", None, None, None)),
        out_specs=(P("dp", None, None, None), P(), P()),
        check_vma=False,
    )
```

```python
import functools
import math

import jax
import jax.numpy as jnp
from jax import lax
from jax.experimental import pallas as pl
from jax.experimental.pallas import tpu as pltpu
from jax.sharding import PartitionSpec as P

LANES = 128


def bit_order(chunk, levels):
    middle = list(range(1, levels - 1))
    turn = chunk % max(1, len(middle))
    return [0] + middle[turn:] + middle[:turn] + [levels - 1]


def sum_kernel(
    levels,
    width,
    ext_ref,
    pre_ref,
    tail_ref,
    carried_ref,
    two_ref,
    out_ref,
    acc,
    sent,
    came,
    taps,
    turned,
    dpre,
    rs_send,
    rs_recv,
    ag_send,
    ag_recv,
):
    chunks, rows = (acc.shape[0], acc.shape[1])
    count, pixels, inner = pre_ref.shape
    channels = ext_ref.shape[2]
    real = two_ref.shape[0]
    me = lax.axis_index("dp")
    bits = [lax.rem(me // (1 << k), 2) for k in range(levels)]
    partners = [me + (1 - 2 * bits[k]) * (1 << k) for k in range(levels)]
    orders = [bit_order(chunk, levels) for chunk in range(chunks)]

    barrier = pltpu.get_barrier_semaphore()
    for k in range(levels):
        pl.semaphore_signal(barrier, inc=1, device_id=(partners[k],), device_id_type=pl.DeviceIdType.MESH)

    for chunk in range(chunks):
        if chunk:
            acc[chunk, :real, :] = two_ref[:, (chunk - 1) * LANES : chunk * LANES]
        if rows > real:
            acc[chunk, real:, :] = jnp.zeros((rows - real, LANES), jnp.float32)

    pl.semaphore_wait(barrier, levels)

    def aligned(value):
        return pl.multiple_of(value, 16)

    def landing(chunk, base, size):
        at = pl.ds(aligned(base), size)
        return out_ref.at[chunk, at]

    def scatter_copy(chunk, step):
        size = rows >> (step + 1)
        at = rows - (rows >> step)
        return pltpu.make_async_remote_copy(
            src_ref=sent.at[chunk, pl.ds(at, size)],
            dst_ref=came.at[chunk, pl.ds(at, size)],
            send_sem=rs_send.at[chunk, step],
            recv_sem=rs_recv.at[chunk, step],
            device_id=(partners[orders[chunk][step]],),
            device_id_type=pl.DeviceIdType.MESH,
        )

    def gather_copy(chunk, step, base):
        size = rows >> (step + 1)
        return pltpu.make_async_remote_copy(
            src_ref=landing(chunk, base, size),
            dst_ref=landing(chunk, base, size),
            send_sem=ag_send.at[chunk, step],
            recv_sem=ag_recv.at[chunk, step],
            device_id=(partners[orders[chunk][step]],),
            device_id_type=pl.DeviceIdType.MESH,
        )

    base = [jnp.int32(0)] * chunks
    copies = [None] * chunks
    pending = []

    def start(chunk, copy):
        copies[chunk] = copy
        copy.start()
        pending.append(copy)

    def send_half(chunk, step):
        size = rows >> (step + 1)
        at = rows - (rows >> step)
        bit = bits[orders[chunk][step]]
        away = aligned(base[chunk] + (1 - bit) * size)
        sent[chunk, pl.ds(at, size), :] = acc[chunk, pl.ds(away, size), :].astype(jnp.bfloat16)
        start(chunk, scatter_copy(chunk, step))
        base[chunk] = base[chunk] + bit * size

    def scatter_step(chunk, step):
        size = rows >> (step + 1)
        at = rows - (rows >> step)
        copies[chunk].wait_recv()
        here = pl.ds(aligned(base[chunk]), size)
        total = acc[chunk, here, :] + came[chunk, pl.ds(at, size), :].astype(jnp.float32)
        if step + 1 < levels:
            acc[chunk, here, :] = total
            send_half(chunk, step + 1)
        else:
            landing(chunk, base[chunk], size)[...] = total.astype(jnp.bfloat16)
            start(chunk, gather_copy(chunk, step, base[chunk]))

    def gather_step(chunk, step):
        size = rows >> (step + 1)
        copies[chunk].wait_recv()
        base[chunk] = base[chunk] - bits[orders[chunk][step]] * size
        if step > 0:
            start(chunk, gather_copy(chunk, step - 1, base[chunk]))

    def steps(chunk):
        work = [functools.partial(send_half, chunk, 0)]
        work += [functools.partial(scatter_step, chunk, step) for step in range(levels)]
        return work + [functools.partial(gather_step, chunk, step) for step in reversed(range(levels))]

    def slope_part():
        @pl.loop(0, count)
        def _(f):
            dhid = tail_ref[f]
            more = carried_ref[jnp.maximum(f - (count - 2), 0)].astype(jnp.float32)
            dhid = dhid + jnp.where(jnp.broadcast_to(f >= count - 2, more.shape), more, 0.0)
            at = pl.ds(pl.multiple_of(f * pixels, pixels), pixels)
            dpre[at, :] = (dhid * silu_slope(pre_ref[f])).astype(jnp.bfloat16)

    def outer_part(kt):
        height = turned.shape[0] // 3

        @pl.loop(0, 3)
        def _(kh):
            at = pl.ds(pl.multiple_of(kh * height, height), height)
            into = pl.ds(pl.multiple_of((kt * 3 + kh) * height, height), height)
            acc[0, into, :] = jnp.dot(
                turned[at, kt * pixels : kt * pixels + count * pixels], dpre[...], preferred_element_type=jnp.float32
            )

    local = [
        functools.partial(spread, ext_ref.at[pl.ds(2, count + 2)], taps, width),
        functools.partial(turn, taps, 0, turned, channels),
        slope_part,
    ] + [functools.partial(outer_part, kt) for kt in range(3)]
    queues = [steps(chunk) for chunk in range(chunks)]
    for part in local:
        part()
    while any(queues):
        for chunk in range(chunks):
            if queues[chunk]:
                queues[chunk].pop(0)()
    for copy in pending:
        copy.wait_send()


def sum_over_devices(width, ext, pre, tail, carried, two):
    devices = lax.axis_size("dp")
    levels = devices.bit_length() - 1
    assert devices == 1 << levels
    count, pixels, inner = pre.shape
    channels = ext.shape[2]
    assert inner == LANES
    two = two.reshape(-1, two.shape[-1])
    real, wide = two.shape
    step = 16 * devices
    rows = -(-real // step) * step
    chunks = 1 + wide // LANES
    summed = pl.pallas_call(
        functools.partial(sum_kernel, levels, width),
        out_shape=jax.ShapeDtypeStruct((chunks, rows, LANES), jnp.bfloat16),
        in_specs=[pl.BlockSpec(memory_space=pltpu.VMEM)] * 5,
        out_specs=pl.BlockSpec(memory_space=pltpu.VMEM),
        scratch_shapes=[
            pltpu.VMEM((chunks, rows, LANES), jnp.float32),
            pltpu.VMEM((chunks, rows, LANES), jnp.bfloat16),
            pltpu.VMEM((chunks, rows, LANES), jnp.bfloat16),
            pltpu.VMEM((count + 2, pixels, 9 * channels), jnp.bfloat16),
            pltpu.VMEM((9 * channels, (count + 2) * pixels), jnp.bfloat16),
            pltpu.VMEM((count * pixels, inner), jnp.bfloat16),
        ]
        + [pltpu.SemaphoreType.DMA((chunks, levels))] * 4,
        compiler_params=pltpu.CompilerParams(
            collective_id=0, has_side_effects=True, vmem_limit_bytes=56 * 1024 * 1024
        ),
    )(ext, pre, tail, carried, two)
    summed = summed[:, :real].astype(jnp.float32)
    return summed[0], jnp.concatenate([summed[chunk] for chunk in range(1, chunks)], axis=1)


def from_behind(value, axis, steps):
    count = lax.axis_size(axis)
    initial, last = (max(0, -steps), min(count, count - steps))
    return lax.ppermute(value, axis, [(source, source + steps) for source in range(initial, last)])


def spread(source, target, width):
    count, pixels, channels = source.shape
    column = lax.broadcasted_iota(jnp.int32, (pixels, channels), 0) % width

    @pl.loop(0, count)
    def _(f):
        value = source[f]
        wide = value.astype(jnp.float32)
        left = jnp.where(column == 0, 0.0, pltpu.roll(wide, 1, 0)).astype(jnp.bfloat16)
        right = jnp.where(column == width - 1, 0.0, pltpu.roll(wide, pixels - 1, 0)).astype(jnp.bfloat16)
        blank = jnp.zeros((width, channels), jnp.bfloat16)
        for kw, moved in enumerate((left, value, right)):
            target[f, :, (3 + kw) * channels : (4 + kw) * channels] = moved
            cols = slice(kw * channels, (kw + 1) * channels)
            target[f, width:, cols] = moved[: pixels - width]
            target[f, :width, cols] = blank
            cols = slice((6 + kw) * channels, (7 + kw) * channels)
            target[f, : pixels - width, cols] = moved[width:]
            target[f, pixels - width :, cols] = blank


def turn(taps, first, turned, channels):
    pixels = taps.shape[1]

    @pl.loop(0, turned.shape[1] // pixels)
    def _(f):
        at = pl.ds(pl.multiple_of(f * pixels, pixels), pixels)
        for tap in range(9):
            cols = slice(tap * channels, (tap + 1) * channels)
            turned[cols, at] = taps[first + f, :, cols].T


def outer(turned, grad, result, pixels):
    rows = grad.shape[0]
    height = turned.shape[0] // 3
    for kt in range(3):

        @pl.loop(0, 3)
        def _(kh):
            at = pl.ds(pl.multiple_of(kh * height, height), height)
            result[kt, at, :] = jnp.dot(
                turned[at, kt * pixels : kt * pixels + rows], grad[...], preferred_element_type=jnp.float32
            )


def clip_place(blocks_ref, tails_ref, count):
    place = lax.axis_index("dp")
    start, keep, valid = (jnp.int32(0), jnp.int32(1), jnp.int32(count))
    for clip in range(blocks_ref.shape[0]):
        keep = jnp.where(start == place, 0, keep)
        start = start + blocks_ref[clip]
        valid = jnp.where(start - 1 == place, tails_ref[clip], valid)
    return keep, valid


def back_kernel(width, scale, blocks_ref, tails_ref, cot_ref, weight_ref, dout_ref, head_ref, tail_ref, taps, flipped, back):
    count, pixels, channels = cot_ref.shape
    inner = tail_ref.shape[2]
    keep, valid = clip_place(blocks_ref, tails_ref, count)

    @pl.loop(0, count)
    def _(f):
        used = jnp.where(f < valid, jnp.float32(1.0), jnp.float32(0.0))
        dout_ref[f] = ((cot_ref[f].astype(jnp.float32) * used) * scale).astype(jnp.bfloat16)

    spread(dout_ref, taps, width)
    for kt in range(3):
        for tap in range(9):
            flipped[tap * channels : (tap + 1) * channels, kt * inner : (kt + 1) * inner] = weight_ref[kt, 8 - tap].T
    back[...] = jnp.zeros_like(back)

    @pl.loop(0, count // 2)
    def _(g):
        f = g * 2
        part = jnp.dot(
            taps[pl.ds(f, 2)].reshape(2 * pixels, 9 * channels), flipped[...], preferred_element_type=jnp.float32
        ).reshape(2, pixels, 3 * inner)
        for kt in range(3):
            back[pl.ds(f + kt, 2)] += part[:, :, kt * inner : (kt + 1) * inner]

    held = jnp.where(keep > 0, jnp.float32(1.0), jnp.float32(0.0))
    head_ref[...] = (back[:2] * held).astype(jnp.bfloat16)
    tail_ref[...] = back[2:]


def forward_kernel(
    width,
    blocks_ref,
    tails_ref,
    arrived_ref,
    frames_ref,
    one_ref,
    two_ref,
    dout_ref,
    feat_ref,
    pre_ref,
    grad_ref,
    ext_ref,
    taps,
    turned,
    pre,
    hidden,
):
    total, pixels, channels = ext_ref.shape
    count = total - 4
    inner = one_ref.shape[2]
    outer_channels = two_ref.shape[2]
    keep, valid = clip_place(blocks_ref, tails_ref, count)
    arrived = arrived_ref[...].astype(jnp.float32) * jnp.where(keep > 0, jnp.float32(1.0), jnp.float32(0.0))
    ext_ref[:4] = arrived.astype(jnp.bfloat16)
    ext_ref[4:] = frames_ref[...]
    spread(ext_ref, taps, width)
    pre[...] = jnp.zeros_like(pre)

    @pl.loop(0, total // 2)
    def _(g):
        f = g * 2
        weight = jnp.concatenate([one_ref[0], one_ref[1], one_ref[2]], axis=1)
        part = jnp.dot(
            taps[pl.ds(f, 2)].reshape(2 * pixels, 9 * channels), weight, preferred_element_type=jnp.float32
        ).reshape(2, pixels, 3 * inner)
        for kt in range(3):
            pre[pl.ds(f + 2 - kt, 2)] += part[:, :, kt * inner : (kt + 1) * inner]

    pre_ref[...] = pre[4 : 4 + count]

    @pl.loop(0, count + 2)
    def _(f):
        value = pre[f + 2]
        held = jnp.where((f >= 2) | (keep > 0), jnp.float32(1.0), jnp.float32(0.0))
        hidden[f] = (jax.nn.silu(value) * held).astype(jnp.bfloat16)

    spread(hidden, taps, width)

    @pl.loop(0, count // 2)
    def _(g):
        f = g * 2
        total_out = jnp.zeros((2 * pixels, outer_channels), jnp.float32)
        for kt in range(3):
            total_out += jnp.dot(
                taps[pl.ds(f + kt, 2)].reshape(2 * pixels, 9 * inner), two_ref[kt], preferred_element_type=jnp.float32
            )
        total_out = total_out.reshape(2, pixels, outer_channels)
        for i in range(2):
            used = jnp.broadcast_to(f + i < valid, (pixels, outer_channels))
            feat_ref[f + i] = jnp.where(used, total_out[i], 0.0).astype(jnp.bfloat16)

    turn(taps, 0, turned, inner)
    outer(turned, dout_ref, grad_ref, pixels)


def silu_slope(value):
    sig = jax.nn.sigmoid(value)
    return sig * (1.0 + value * (1.0 - sig))


VMEM = pl.BlockSpec(memory_space=pltpu.VMEM)
SMEM = pl.BlockSpec(memory_space=pltpu.SMEM)
PARAMS = pltpu.CompilerParams(vmem_limit_bytes=56 * 1024 * 1024)


def local(frames, clip_blocks, tail_frames, weight_one, weight_two, cotangent):
    count, height, width, channels = frames.shape
    pixels = height * width
    inner = weight_one.shape[-1]
    wide = weight_two.shape[-1]
    bf16, f32 = (jnp.bfloat16, jnp.float32)
    devices = lax.axis_size("dp")
    frames = frames.reshape(count, pixels, channels)
    cotangent = cotangent.reshape(count, pixels, wide)
    one = weight_one.reshape(3, 9 * channels, inner)
    arrived = from_behind(frames[count - 4 :], "dp", 1)
    scale = 1.0 / math.sqrt(devices * count * pixels)

    dout, head, tail = pl.pallas_call(
        functools.partial(back_kernel, width, scale),
        out_shape=(
            jax.ShapeDtypeStruct((count, pixels, wide), bf16),
            jax.ShapeDtypeStruct((2, pixels, inner), bf16),
            jax.ShapeDtypeStruct((count, pixels, inner), f32),
        ),
        in_specs=[SMEM, SMEM, VMEM, VMEM],
        out_specs=(VMEM, VMEM, VMEM),
        scratch_shapes=[
            pltpu.VMEM((count, pixels, 9 * wide), bf16),
            pltpu.VMEM((9 * wide, 3 * inner), bf16),
            pltpu.VMEM((count + 2, pixels, inner), f32),
        ],
        compiler_params=PARAMS,
        cost_estimate=pl.CostEstimate(flops=10**10, bytes_accessed=5 * 10**6, transcendentals=0),
    )(clip_blocks, tail_frames, cotangent, weight_two.reshape(3, 9, inner, wide))
    carried = from_behind(head, "dp", -1)
    features, pre, grad_two, ext = pl.pallas_call(
        functools.partial(forward_kernel, width),
        out_shape=(
            jax.ShapeDtypeStruct((count, pixels, wide), bf16),
            jax.ShapeDtypeStruct((count, pixels, inner), f32),
            jax.ShapeDtypeStruct((3, 9 * inner, wide), f32),
            jax.ShapeDtypeStruct((count + 4, pixels, channels), bf16),
        ),
        in_specs=[SMEM, SMEM, VMEM, VMEM, VMEM, VMEM, VMEM],
        out_specs=(VMEM, VMEM, VMEM, VMEM),
        scratch_shapes=[
            pltpu.VMEM((count + 4, pixels, 9 * max(channels, inner)), bf16),
            pltpu.VMEM((9 * inner, (count + 2) * pixels), bf16),
            pltpu.VMEM((count + 6, pixels, inner), f32),
            pltpu.VMEM((count + 2, pixels, inner), bf16),
        ],
        compiler_params=PARAMS,
        cost_estimate=pl.CostEstimate(flops=12 * 10**9, bytes_accessed=12 * 10**6, transcendentals=0),
    )(clip_blocks, tail_frames, arrived, frames, one, weight_two.reshape(3, 9 * inner, wide), dout.reshape(count * pixels, wide))
    grad_one, grad_two = sum_over_devices(width, ext, pre, tail, carried, grad_two)
    return (
        features.reshape(count, height, width, wide),
        grad_one.reshape(weight_one.shape),
        grad_two.reshape(weight_two.shape),
    )


def solution(mesh):
    return jax.shard_map(
        local,
        mesh=mesh,
        in_specs=(P("dp", None, None, None), P(), P(), P(), P(), P("dp", None, None, None)),
        out_specs=(P("dp", None, None, None), P(), P()),
        check_vma=False,
    )
```

```python
import functools
import math

import jax
import jax.numpy as jnp
from jax import lax
from jax.experimental import pallas as pl
from jax.experimental.pallas import tpu as pltpu
from jax.sharding import PartitionSpec as P

LANES = 128


def bit_order(chunk, levels):
    middle = list(range(1, levels - 1))
    turn = chunk % max(1, len(middle))
    return [0] + middle[turn:] + middle[:turn] + [levels - 1]


def sum_kernel(levels, one_ref, two_ref, out_ref, acc, sent, came, rs_send, rs_recv, ag_send, ag_recv):
    chunks, rows = (acc.shape[0], acc.shape[1])
    real = one_ref.shape[0]
    me = lax.axis_index("dp")
    bits = [lax.rem(me // (1 << k), 2) for k in range(levels)]
    partners = [me + (1 - 2 * bits[k]) * (1 << k) for k in range(levels)]
    orders = [bit_order(chunk, levels) for chunk in range(chunks)]

    barrier = pltpu.get_barrier_semaphore()
    for k in range(levels):
        pl.semaphore_signal(barrier, inc=1, device_id=(partners[k],), device_id_type=pl.DeviceIdType.MESH)

    wide = one_ref.shape[1] // LANES
    for chunk in range(chunks):
        ref, col = (one_ref, chunk) if chunk < wide else (two_ref, chunk - wide)
        acc[chunk, :real, :] = ref[:, col * LANES : (col + 1) * LANES]
        if rows > real:
            acc[chunk, real:, :] = jnp.zeros((rows - real, LANES), jnp.float32)

    pl.semaphore_wait(barrier, levels)

    def aligned(value):
        return pl.multiple_of(value, 16)

    def scatter_copy(chunk, step):
        size = rows >> (step + 1)
        at = rows - (rows >> step)
        return pltpu.make_async_remote_copy(
            src_ref=sent.at[chunk, pl.ds(at, size)],
            dst_ref=came.at[chunk, pl.ds(at, size)],
            send_sem=rs_send.at[chunk, step],
            recv_sem=rs_recv.at[chunk, step],
            device_id=(partners[orders[chunk][step]],),
            device_id_type=pl.DeviceIdType.MESH,
        )

    def gather_copy(chunk, step, base):
        size = rows >> (step + 1)
        return pltpu.make_async_remote_copy(
            src_ref=out_ref.at[chunk, pl.ds(aligned(base), size)],
            dst_ref=out_ref.at[chunk, pl.ds(aligned(base), size)],
            send_sem=ag_send.at[chunk, step],
            recv_sem=ag_recv.at[chunk, step],
            device_id=(partners[orders[chunk][step]],),
            device_id_type=pl.DeviceIdType.MESH,
        )

    base = [jnp.int32(0)] * chunks
    copies = [None] * chunks
    pending = []

    def send_half(chunk, step):
        size = rows >> (step + 1)
        at = rows - (rows >> step)
        bit = bits[orders[chunk][step]]
        away = aligned(base[chunk] + (1 - bit) * size)
        sent[chunk, pl.ds(at, size), :] = acc[chunk, pl.ds(away, size), :].astype(jnp.bfloat16)
        copies[chunk] = scatter_copy(chunk, step)
        copies[chunk].start()
        pending.append(copies[chunk])
        base[chunk] = base[chunk] + bit * size

    for chunk in range(chunks):
        send_half(chunk, 0)
    for step in range(levels):
        size = rows >> (step + 1)
        at = rows - (rows >> step)
        for chunk in range(chunks):
            copies[chunk].wait_recv()
            here = pl.ds(aligned(base[chunk]), size)
            total = acc[chunk, here, :] + came[chunk, pl.ds(at, size), :].astype(jnp.float32)
            if step + 1 < levels:
                acc[chunk, here, :] = total
                send_half(chunk, step + 1)
            else:
                out_ref[chunk, here, :] = total.astype(jnp.bfloat16)
                copies[chunk] = gather_copy(chunk, step, base[chunk])
                copies[chunk].start()
                pending.append(copies[chunk])
    for step in reversed(range(levels)):
        size = rows >> (step + 1)
        for chunk in range(chunks):
            copies[chunk].wait_recv()
            base[chunk] = base[chunk] - bits[orders[chunk][step]] * size
            if step > 0:
                copies[chunk] = gather_copy(chunk, step - 1, base[chunk])
                copies[chunk].start()
                pending.append(copies[chunk])
    for copy in pending:
        copy.wait_send()


def sum_over_devices(one, two):
    devices = lax.axis_size("dp")
    levels = devices.bit_length() - 1
    assert devices == 1 << levels
    shape_one, shape_two = (one.shape, two.shape)
    one = one.reshape(-1, one.shape[-1])
    two = two.reshape(-1, two.shape[-1])
    real = one.shape[0]
    step = 16 * devices
    rows = -(-real // step) * step
    chunks = (one.shape[1] + two.shape[1]) // LANES
    summed = pl.pallas_call(
        functools.partial(sum_kernel, levels),
        out_shape=jax.ShapeDtypeStruct((chunks, rows, LANES), jnp.bfloat16),
        in_specs=[pl.BlockSpec(memory_space=pltpu.VMEM)] * 2,
        out_specs=pl.BlockSpec(memory_space=pltpu.VMEM),
        scratch_shapes=[
            pltpu.VMEM((chunks, rows, LANES), jnp.float32),
            pltpu.VMEM((chunks, rows, LANES), jnp.bfloat16),
            pltpu.VMEM((chunks, rows, LANES), jnp.bfloat16),
        ]
        + [pltpu.SemaphoreType.DMA((chunks, levels))] * 4,
        compiler_params=pltpu.CompilerParams(
            collective_id=0, has_side_effects=True, vmem_limit_bytes=40 * 1024 * 1024
        ),
    )(one, two)
    summed = summed[:, :real].astype(jnp.float32)
    wide = one.shape[1] // LANES
    whole = [summed[chunk] for chunk in range(chunks)]
    grad_one = jnp.concatenate(whole[:wide], axis=1).reshape(shape_one)
    grad_two = jnp.concatenate(whole[wide:], axis=1).reshape(shape_two)
    return grad_one, grad_two


def from_behind(value, axis, steps):
    count = lax.axis_size(axis)
    initial, last = (max(0, -steps), min(count, count - steps))
    return lax.ppermute(value, axis, [(source, source + steps) for source in range(initial, last)])


def spread(source, target, width):
    count, pixels, channels = source.shape
    column = lax.broadcasted_iota(jnp.int32, (pixels, channels), 0) % width

    @pl.loop(0, count)
    def _(f):
        value = source[f]
        wide = value.astype(jnp.float32)
        left = jnp.where(column == 0, 0.0, pltpu.roll(wide, 1, 0)).astype(jnp.bfloat16)
        right = jnp.where(column == width - 1, 0.0, pltpu.roll(wide, pixels - 1, 0)).astype(jnp.bfloat16)
        blank = jnp.zeros((width, channels), jnp.bfloat16)
        for kw, moved in enumerate((left, value, right)):
            target[f, :, (3 + kw) * channels : (4 + kw) * channels] = moved
            cols = slice(kw * channels, (kw + 1) * channels)
            target[f, width:, cols] = moved[: pixels - width]
            target[f, :width, cols] = blank
            cols = slice((6 + kw) * channels, (7 + kw) * channels)
            target[f, : pixels - width, cols] = moved[width:]
            target[f, pixels - width :, cols] = blank


def turn(taps, first, turned, channels):
    pixels = taps.shape[1]

    @pl.loop(0, turned.shape[1] // pixels)
    def _(f):
        at = pl.ds(pl.multiple_of(f * pixels, pixels), pixels)
        for tap in range(9):
            cols = slice(tap * channels, (tap + 1) * channels)
            turned[cols, at] = taps[first + f, :, cols].T


def outer(turned, grad, result, pixels):
    rows = grad.shape[0]
    height = turned.shape[0] // 3
    for kt in range(3):

        @pl.loop(0, 3)
        def _(kh):
            at = pl.ds(pl.multiple_of(kh * height, height), height)
            result[kt, at, :] = jnp.dot(
                turned[at, kt * pixels : kt * pixels + rows], grad[...], preferred_element_type=jnp.float32
            )


def clip_place(blocks_ref, tails_ref, count):
    place = lax.axis_index("dp")
    start, keep, valid = (jnp.int32(0), jnp.int32(1), jnp.int32(count))
    for clip in range(blocks_ref.shape[0]):
        keep = jnp.where(start == place, 0, keep)
        start = start + blocks_ref[clip]
        valid = jnp.where(start - 1 == place, tails_ref[clip], valid)
    return keep, valid


def back_kernel(width, scale, blocks_ref, tails_ref, cot_ref, weight_ref, dout_ref, head_ref, tail_ref, taps, flipped, back):
    count, pixels, channels = cot_ref.shape
    inner = tail_ref.shape[2]
    keep, valid = clip_place(blocks_ref, tails_ref, count)

    @pl.loop(0, count)
    def _(f):
        used = jnp.where(f < valid, jnp.float32(1.0), jnp.float32(0.0))
        dout_ref[f] = ((cot_ref[f].astype(jnp.float32) * used) * scale).astype(jnp.bfloat16)

    spread(dout_ref, taps, width)
    for kt in range(3):
        for tap in range(9):
            flipped[tap * channels : (tap + 1) * channels, kt * inner : (kt + 1) * inner] = weight_ref[kt, 8 - tap].T
    back[...] = jnp.zeros_like(back)

    @pl.loop(0, count // 2)
    def _(g):
        f = g * 2
        part = jnp.dot(
            taps[pl.ds(f, 2)].reshape(2 * pixels, 9 * channels), flipped[...], preferred_element_type=jnp.float32
        ).reshape(2, pixels, 3 * inner)
        for kt in range(3):
            back[pl.ds(f + kt, 2)] += part[:, :, kt * inner : (kt + 1) * inner]

    held = jnp.where(keep > 0, jnp.float32(1.0), jnp.float32(0.0))
    head_ref[...] = (back[:2] * held).astype(jnp.bfloat16)
    tail_ref[...] = back[2:]


def forward_kernel(
    width,
    blocks_ref,
    tails_ref,
    arrived_ref,
    frames_ref,
    one_ref,
    two_ref,
    dout_ref,
    feat_ref,
    pre_ref,
    grad_ref,
    ext_ref,
    taps,
    turned,
    pre,
    hidden,
):
    total, pixels, channels = ext_ref.shape
    count = total - 4
    inner = one_ref.shape[2]
    outer_channels = two_ref.shape[2]
    keep, valid = clip_place(blocks_ref, tails_ref, count)
    arrived = arrived_ref[...].astype(jnp.float32) * jnp.where(keep > 0, jnp.float32(1.0), jnp.float32(0.0))
    ext_ref[:4] = arrived.astype(jnp.bfloat16)
    ext_ref[4:] = frames_ref[...]
    spread(ext_ref, taps, width)
    pre[...] = jnp.zeros_like(pre)

    @pl.loop(0, total // 2)
    def _(g):
        f = g * 2
        weight = jnp.concatenate([one_ref[0], one_ref[1], one_ref[2]], axis=1)
        part = jnp.dot(
            taps[pl.ds(f, 2)].reshape(2 * pixels, 9 * channels), weight, preferred_element_type=jnp.float32
        ).reshape(2, pixels, 3 * inner)
        for kt in range(3):
            pre[pl.ds(f + 2 - kt, 2)] += part[:, :, kt * inner : (kt + 1) * inner]

    pre_ref[...] = pre[4 : 4 + count]

    @pl.loop(0, count + 2)
    def _(f):
        value = pre[f + 2]
        held = jnp.where((f >= 2) | (keep > 0), jnp.float32(1.0), jnp.float32(0.0))
        hidden[f] = (jax.nn.silu(value) * held).astype(jnp.bfloat16)

    spread(hidden, taps, width)

    @pl.loop(0, count // 2)
    def _(g):
        f = g * 2
        total_out = jnp.zeros((2 * pixels, outer_channels), jnp.float32)
        for kt in range(3):
            total_out += jnp.dot(
                taps[pl.ds(f + kt, 2)].reshape(2 * pixels, 9 * inner), two_ref[kt], preferred_element_type=jnp.float32
            )
        total_out = total_out.reshape(2, pixels, outer_channels)
        for i in range(2):
            used = jnp.broadcast_to(f + i < valid, (pixels, outer_channels))
            feat_ref[f + i] = jnp.where(used, total_out[i], 0.0).astype(jnp.bfloat16)

    turn(taps, 0, turned, inner)
    outer(turned, dout_ref, grad_ref, pixels)


def last_kernel(width, ext_ref, pre_ref, tail_ref, carried_ref, grad_ref, taps, turned, dpre):
    count, pixels, inner = pre_ref.shape
    channels = ext_ref.shape[2]
    spread(ext_ref.at[pl.ds(2, count + 2)], taps, width)
    turn(taps, 0, turned, channels)

    @pl.loop(0, count)
    def _(f):
        dhid = tail_ref[f]
        more = carried_ref[jnp.maximum(f - (count - 2), 0)].astype(jnp.float32)
        dhid = dhid + jnp.where(jnp.broadcast_to(f >= count - 2, more.shape), more, 0.0)
        at = pl.ds(pl.multiple_of(f * pixels, pixels), pixels)
        dpre[at, :] = (dhid * silu_slope(pre_ref[f])).astype(jnp.bfloat16)

    outer(turned, dpre, grad_ref, pixels)


def silu_slope(value):
    sig = jax.nn.sigmoid(value)
    return sig * (1.0 + value * (1.0 - sig))


VMEM = pl.BlockSpec(memory_space=pltpu.VMEM)
SMEM = pl.BlockSpec(memory_space=pltpu.SMEM)
PARAMS = pltpu.CompilerParams(vmem_limit_bytes=56 * 1024 * 1024)


def local(frames, clip_blocks, tail_frames, weight_one, weight_two, cotangent):
    count, height, width, channels = frames.shape
    pixels = height * width
    inner = weight_one.shape[-1]
    wide = weight_two.shape[-1]
    bf16, f32 = (jnp.bfloat16, jnp.float32)
    devices = lax.axis_size("dp")
    frames = frames.reshape(count, pixels, channels)
    cotangent = cotangent.reshape(count, pixels, wide)
    one = weight_one.reshape(3, 9 * channels, inner)
    arrived = from_behind(frames[count - 4 :], "dp", 1)
    scale = 1.0 / math.sqrt(devices * count * pixels)

    dout, head, tail = pl.pallas_call(
        functools.partial(back_kernel, width, scale),
        out_shape=(
            jax.ShapeDtypeStruct((count, pixels, wide), bf16),
            jax.ShapeDtypeStruct((2, pixels, inner), bf16),
            jax.ShapeDtypeStruct((count, pixels, inner), f32),
        ),
        in_specs=[SMEM, SMEM, VMEM, VMEM],
        out_specs=(VMEM, VMEM, VMEM),
        scratch_shapes=[
            pltpu.VMEM((count, pixels, 9 * wide), bf16),
            pltpu.VMEM((9 * wide, 3 * inner), bf16),
            pltpu.VMEM((count + 2, pixels, inner), f32),
        ],
        compiler_params=PARAMS,
        cost_estimate=pl.CostEstimate(flops=10**10, bytes_accessed=5 * 10**6, transcendentals=0),
    )(clip_blocks, tail_frames, cotangent, weight_two.reshape(3, 9, inner, wide))
    carried = from_behind(head, "dp", -1)
    features, pre, grad_two, ext = pl.pallas_call(
        functools.partial(forward_kernel, width),
        out_shape=(
            jax.ShapeDtypeStruct((count, pixels, wide), bf16),
            jax.ShapeDtypeStruct((count, pixels, inner), f32),
            jax.ShapeDtypeStruct((3, 9 * inner, wide), f32),
            jax.ShapeDtypeStruct((count + 4, pixels, channels), bf16),
        ),
        in_specs=[SMEM, SMEM, VMEM, VMEM, VMEM, VMEM, VMEM],
        out_specs=(VMEM, VMEM, VMEM, VMEM),
        scratch_shapes=[
            pltpu.VMEM((count + 4, pixels, 9 * max(channels, inner)), bf16),
            pltpu.VMEM((9 * inner, (count + 2) * pixels), bf16),
            pltpu.VMEM((count + 6, pixels, inner), f32),
            pltpu.VMEM((count + 2, pixels, inner), bf16),
        ],
        compiler_params=PARAMS,
        cost_estimate=pl.CostEstimate(flops=12 * 10**9, bytes_accessed=12 * 10**6, transcendentals=0),
    )(clip_blocks, tail_frames, arrived, frames, one, weight_two.reshape(3, 9 * inner, wide), dout.reshape(count * pixels, wide))
    grad_one = pl.pallas_call(
        functools.partial(last_kernel, width),
        out_shape=jax.ShapeDtypeStruct((3, 9 * channels, inner), f32),
        in_specs=[VMEM] * 4,
        out_specs=VMEM,
        scratch_shapes=[
            pltpu.VMEM((count + 2, pixels, 9 * channels), bf16),
            pltpu.VMEM((9 * channels, (count + 2) * pixels), bf16),
            pltpu.VMEM((count * pixels, inner), bf16),
        ],
        compiler_params=PARAMS,
        cost_estimate=pl.CostEstimate(flops=4 * 10**9, bytes_accessed=5 * 10**6, transcendentals=0),
    )(ext, pre, tail, carried)
    grad_one, grad_two = sum_over_devices(grad_one, grad_two)
    return (
        features.reshape(count, height, width, wide),
        grad_one.reshape(weight_one.shape),
        grad_two.reshape(weight_two.shape),
    )


def solution(mesh):
    return jax.shard_map(
        local,
        mesh=mesh,
        in_specs=(P("dp", None, None, None), P(), P(), P(), P(), P("dp", None, None, None)),
        out_specs=(P("dp", None, None, None), P(), P()),
        check_vma=False,
    )
```
